512 devices in a mesh: section: 16 (over y_lo, x, core), dp: 32 (over y_hi, z).
Axes of the slice: x: 4, y: 8 (y_hi: 4, y_lo: 2; y = y_hi * 2 + y_lo), z: 8, core: 2. Of those that a mesh axis runs over, the one named last changes fastest.
Arguments:
- inputs: bfloat16 [4, 1024, 2560], P(None, 'dp'), may hold values from -6 to 6
- cotangent: bfloat16 [4, 1024, 2560], P(None, 'dp'), may hold values from -4.2 to 4.2
- weight: bfloat16 [16, 2560, 2560], P('section', 'dp'), may hold values from -1 to 1
- gain: float32 [16, 2560], P('section'), may hold values from 0.1 to 1.9
- momentum: float32 [16, 32, 2560], P('section', 'dp'), may hold values from -6 to 6
- prev_grads: float32 [16, 32, 32, 2560], P('section', 'dp'), may hold values from -6 to 6
Outputs:
- input_grads: bfloat16 [16, 4, 1024, 2560], P('section', None, 'dp')
- gain_grads: float32 [16, 32, 2560], P('section', 'dp')
- new_momentum: float32 [16, 32, 2560], P('section', 'dp')
The draws below stay inside these ranges and needn't reach their ends.
All inputs are finite; a program needn't handle non-finite values.
Results may differ from the reference program's by a relative error of at most 0.015.
Values may be sent and summed in bfloat16 or wider, within the bound.
No kernel may reach another device: no remote copies, remote signals or barrier semaphores. Data moves between devices by JAX's collectives and lax.ppermute only.
A program may use at most 64 MiB of HBM per device.

```python
import jax
import jax.numpy as jnp
from jax import lax

D = 2560
BLOCK = 32
MB = 4
SECTIONS = 16
TOKENS = 1024
BUCKET = 32
N_DP = 32


def shared_rows(key):
    values = jax.random.normal(key, (MB, TOKENS, D), jnp.float32)
    return jnp.clip(values, -6.0, 6.0)


def draw_inputs(key, part):
    base = shared_rows(key)
    return base.astype(jnp.bfloat16)


def draw_cotangent(key, part):
    base = shared_rows(key)
    key = jax.random.fold_in(key, 7)
    noise = jnp.clip(jax.random.normal(key, (MB, TOKENS, D), jnp.float32), -6.0, 6.0)
    return (0.4 * base + 0.3 * noise).astype(jnp.bfloat16)


def draw_weight(key, part):
    key = jax.random.fold_in(key, 3)
    first_key, second_key = jax.random.split(key)
    factor = 0.5 / D ** 0.5
    spread_part = jnp.clip(jax.random.normal(first_key, (SECTIONS, D, D), jnp.float32), -6.0, 6.0) * factor
    diagonal = jax.random.uniform(second_key, (SECTIONS, D), jnp.float32, 0.2, 0.4)
    identity = jnp.eye(D, dtype=jnp.float32)
    return (spread_part + diagonal[:, :, None] * identity[None]).astype(jnp.bfloat16)


def spiked(drawn, rng, source, target, parts, factor):
    owner, partner = [(jnp.arange(drawn.shape[position]) // (drawn.shape[position] // parts)).reshape([-1 if axis == position else 1 for axis in range(drawn.ndim)]) for position in (source, target)]
    chosen = jax.random.permutation(rng, parts)[partner]
    strong = (owner == chosen) | (owner == (partner + parts // 2) % parts)
    return jnp.where(strong, factor * drawn, drawn)


def level_of(stream_key, shape, cuts, low, top_value):
    level = 1.0
    for position, shards_of in cuts:
        heights = jax.random.uniform(jax.random.fold_in(jax.random.fold_in(stream_key, 6), position), (shards_of,), jnp.float32, low / len(cuts), top_value / len(cuts))
        level = level * jnp.repeat(jnp.exp(heights), shape[position] // shards_of).reshape((-1,) + (1,) * (len(shape) - 1 - position))
    return level


def bell_draw(own_key, extent, deviation, most, shards=(), held_as=jnp.bfloat16):
    entries = jax.random.normal(own_key, extent, jnp.float32) * deviation
    if len(shards) > 0:
        entries = level_of(own_key, extent, shards, -0.22, 0.18) * entries
    return jnp.clip(entries, min=-most, max=most).astype(held_as)


def heavy_noise(own_key, shape, scale, most, shards, heavy, kind=jnp.bfloat16):
    result = scale * jax.random.normal(own_key, shape, jnp.float32)
    if shards:
        result = result * level_of(own_key, shape, shards, -0.22, 0.18)
    return jnp.clip(spiked(result, jax.random.fold_in(own_key, 3), *heavy), -most, most).astype(kind)


def setup_inputs(seed: int = 0) -> dict:
    key_of = jax.random.split(jax.random.key(seed), 7)
    return {
        "inputs": draw_inputs(jax.random.fold_in(key_of[6], 71), 0),
        "cotangent": draw_cotangent(jax.random.fold_in(key_of[6], 71), 0),
        "weight": draw_weight(jax.random.fold_in(key_of[6], 71), 0),
        "gain": jnp.clip(1.0 + 0.18 * jax.random.normal(key_of[3], (SECTIONS, D), jnp.float32), 0.1, 1.9),
        "momentum": bell_draw(key_of[4], (SECTIONS, BUCKET, D), 1.0, 6.0, ((0, 16), (1, 32)), jnp.float32),
        "prev_grads": heavy_noise(key_of[5], (SECTIONS, N_DP, BUCKET, D), 1.0, 6.0, ((0, 16), (1, 32)), (1, 2, 32, 2.75), jnp.float32),
    }


def normalize(acts):
    values = acts.astype(jnp.float32)
    center = values - lax.optimization_barrier(jnp.mean(values, axis=-1, keepdims=True))
    variance = lax.optimization_barrier(jnp.mean(center * center, axis=-1, keepdims=True))
    inverse = 1.0 / jnp.sqrt(variance + 1e-05)
    return (center * inverse, inverse)

def reference(inputs, cotangent, weight, gain, momentum, prev_grads):
    acts = inputs.reshape(MB * TOKENS, D)
    stashed = []
    for section_num in range(SECTIONS):
        normed, inverse = normalize(acts)
        scaled_in = (normed * gain[section_num]).astype(jnp.bfloat16)
        projected = jnp.dot(scaled_in, weight[section_num], preferred_element_type=jnp.float32)
        stashed.append(acts)
        acts = (acts.astype(jnp.float32) + projected).astype(jnp.bfloat16)
    grad = cotangent.reshape(MB * TOKENS, D)
    grad_list = [None] * SECTIONS
    gain_list = [None] * SECTIONS
    for section_num in range(SECTIONS - 1, -1, -1):
        normed, inverse = normalize(stashed[section_num])
        back_proj = jnp.dot(grad, weight[section_num].T, preferred_element_type=jnp.float32)
        scaled = back_proj * gain[section_num]
        mean_one = lax.optimization_barrier(jnp.mean(scaled, axis=-1, keepdims=True))
        mean_two = lax.optimization_barrier(jnp.mean(scaled * normed, axis=-1, keepdims=True))
        norm_grad = inverse * (scaled - mean_one - normed * mean_two)
        product = (back_proj * normed).reshape(MB, N_DP, BLOCK, D)
        gain_list[section_num] = lax.optimization_barrier(jnp.sum(product, axis=(0, 2)))
        grad = (grad.astype(jnp.float32) + norm_grad).astype(jnp.bfloat16)
        grad_list[section_num] = grad.reshape(MB, TOKENS, D)
    input_grads = jnp.stack(grad_list)
    gain_grads = jnp.stack(gain_list)
    new_momentum = 0.9 * momentum + lax.optimization_barrier(jnp.sum(prev_grads, axis=1)) / N_DP
    return (input_grads, gain_grads, new_momentum)
```

```python
import functools

import jax
import jax.numpy as jnp
from jax import lax
from jax.experimental import pallas as pl
from jax.experimental.pallas import tpu as pltpu
from jax.sharding import PartitionSpec as P

VMEM = pl.BlockSpec(memory_space=pltpu.VMEM)
BF16 = jnp.bfloat16
F32 = jnp.float32
LIMIT = 20 << 20


def normalize(acts):
    values = acts.astype(F32)
    center = values - jnp.mean(values, axis=-1, keepdims=True)
    variance = jnp.mean(center * center, axis=-1, keepdims=True)
    inverse = 1.0 / jnp.sqrt(variance + 1e-05)
    return center * inverse, inverse


def prepare_kernel(step, source, weight_ref, turned_ref, sems):
    width = source.shape[0]
    count = width // step

    def piece(i):
        here = pl.ds(i * step, step)
        return pltpu.make_async_copy(source.at[here, :], weight_ref.at[here, :], sems.at[i])

    for i in range(count):
        piece(i).start()
    for i in range(count):
        piece(i).wait()

        def turn(j, _):
            across = pl.ds(pl.multiple_of(j * step, step), step)
            turned_ref[across, i * step : (i + 1) * step] = weight_ref[i * step : (i + 1) * step, across].T

        lax.fori_loop(0, count, turn, None)


def prepare(whole):
    step = 256
    return pl.pallas_call(
        functools.partial(prepare_kernel, step),
        out_shape=[pltpu.VMEM(whole.shape, whole.dtype)] * 2,
        in_specs=[pl.BlockSpec(memory_space=pltpu.HBM)],
        out_specs=[VMEM] * 2,
        scratch_shapes=[pltpu.SemaphoreType.DMA((whole.shape[0] // step,))],
        compiler_params=pltpu.CompilerParams(vmem_limit_bytes=LIMIT),
        name="prepare_weight",
    )(whole)


def forward_kernel(tile, x_ref, gain_ref, weight_ref, y_ref, scaled):
    normed, _ = normalize(x_ref[...])
    scaled[...] = (normed * gain_ref[...]).astype(BF16)

    def column(i, _):
        here = pl.ds(pl.multiple_of(i * tile, tile), tile)
        projected = jnp.dot(scaled[...], weight_ref[:, here], preferred_element_type=F32)
        y_ref[:, here] = (x_ref[:, here].astype(F32) + projected).astype(BF16)

    lax.fori_loop(0, x_ref.shape[1] // tile, column, None)


def forward(x, gain, weight):
    rows, width = x.shape
    return pl.pallas_call(
        functools.partial(forward_kernel, width // 2),
        out_shape=jax.ShapeDtypeStruct(x.shape, BF16),
        in_specs=[VMEM] * 3,
        out_specs=VMEM,
        scratch_shapes=[pltpu.VMEM((rows, width), BF16)],
        compiler_params=pltpu.CompilerParams(vmem_limit_bytes=LIMIT),
        name="forward",
    )(x, gain, pltpu.with_memory_space_constraint(weight, pltpu.VMEM))


def backward_kernel(tile, grad_ref, x_ref, gain_ref, total_ref, weight_ref, out_ref, new_total_ref, back):
    def column(i, _):
        here = pl.ds(pl.multiple_of(i * tile, tile), tile)
        back[:, here] = jnp.dot(grad_ref[...], weight_ref[:, here], preferred_element_type=F32)

    lax.fori_loop(0, x_ref.shape[1] // tile, column, None)
    normed, inverse = normalize(x_ref[...])
    back_proj = back[...]
    scaled = back_proj * gain_ref[...]
    mean_one = jnp.mean(scaled, axis=-1, keepdims=True)
    mean_two = jnp.mean(scaled * normed, axis=-1, keepdims=True)
    norm_grad = inverse * (scaled - mean_one - normed * mean_two)
    out_ref[...] = (grad_ref[...].astype(F32) + norm_grad).astype(BF16)
    new_total_ref[...] = total_ref[...] + jnp.sum(back_proj * normed, axis=0, keepdims=True)


def backward(grad, x, gain, total, weight):
    rows, width = x.shape
    return pl.pallas_call(
        functools.partial(backward_kernel, width // 2),
        out_shape=(jax.ShapeDtypeStruct(x.shape, BF16), jax.ShapeDtypeStruct(total.shape, F32)),
        in_specs=[VMEM] * 5,
        out_specs=[VMEM] * 2,
        scratch_shapes=[pltpu.VMEM((rows, width), F32)],
        compiler_params=pltpu.CompilerParams(vmem_limit_bytes=LIMIT),
        name="backward",
    )(grad, x, gain, total, pltpu.with_memory_space_constraint(weight, pltpu.VMEM))


def per_device(inputs, cotangent, weight, gain, momentum, prev_grads):
    sections = lax.axis_size("section")
    section = lax.axis_index("section")
    batches, rows, width = inputs.shape

    whole = lax.all_gather(weight[0], "dp", axis=0, tiled=True)

    bucket = prev_grads[0, 0].astype(BF16)
    pieces = lax.all_to_all(bucket, "dp", 0, 0, tiled=True).astype(F32)
    summed = jnp.sum(pieces, axis=0, keepdims=True)
    new_momentum = 0.9 * momentum + (summed / lax.axis_size("dp"))[None]

    resident, turned = prepare(whole)

    parts = range(batches)
    up = [[(s, s + 1) for s in range(h, sections - 1, 2)] for h in range(2)]
    down = [[(s, s - 1) for s in range(sections - 1 - h, 0, -2)] for h in range(2)]

    def forward_pair(j, carry):
        received, stash = carry
        for h in range(2):
            s = 2 * j + h
            mine = section == s
            runs = jnp.logical_and(mine, section < sections - 1)
            sent = []
            for m in parts:
                y = lax.cond(runs, lambda x: forward(x, gain, resident), lambda x: x, received[m])
                sent.append(lax.ppermute(y, "section", up[h]))
            stash = [jnp.where(mine, received[m], stash[m]) for m in parts]
            received = sent
        return received, stash

    fresh = [inputs[m] for m in parts]
    received, stash = lax.fori_loop(0, sections // 2, forward_pair, (fresh, fresh))

    def backward_pair(j, carry):
        incoming, collected, total = carry
        for h in range(2):
            s = sections - 1 - 2 * j - h
            sent = []
            kept = []
            for m in parts:
                out, total = lax.cond(
                    section == s,
                    lambda grad, x, old, total: tuple(backward(grad, x, gain, total, turned)),
                    lambda grad, x, old, total: (old, total),
                    incoming[m],
                    stash[m],
                    collected[m],
                    total,
                )
                kept.append(out)
                sent.append(lax.ppermute(out, "section", down[h]))
            incoming, collected = sent, kept
        return incoming, collected, total

    start = ([cotangent[m] for m in parts], [jnp.zeros((rows, width), BF16) for m in parts], jnp.zeros((1, width), F32))
    incoming, collected, total = lax.fori_loop(0, sections // 2, backward_pair, start)
    input_grads = jnp.stack(collected)[None]
    return input_grads, total[None], new_momentum


def solution(mesh):
    in_specs = (
        P(None, "dp", None),
        P(None, "dp", None),
        P("section", "dp", None),
        P("section", None),
        P("section", "dp", None),
        P("section", "dp", None, None),
    )
    out_specs = (P("section", None, "dp", None), P("section", "dp", None), P("section", "dp", None))
    return jax.shard_map(per_device, mesh=mesh, in_specs=in_specs, out_specs=out_specs, check_vma=False)
```

```python
import functools

import jax
import jax.numpy as jnp
from jax import lax
from jax.experimental import pallas as pl
from jax.experimental.pallas import tpu as pltpu
from jax.sharding import PartitionSpec as P

VMEM = pl.BlockSpec(memory_space=pltpu.VMEM)
SMEM = pl.BlockSpec(memory_space=pltpu.SMEM)
HBM = pl.BlockSpec(memory_space=pltpu.HBM)
BF16 = jnp.bfloat16
F32 = jnp.float32
LIMIT = 2 << 20


def held(array):
    return pltpu.with_memory_space_constraint(array, pltpu.VMEM)


def place_kernel(step, source, *rest):
    weights, turned, sems = rest[-3:]
    slot = 0 if len(rest) == 3 else 1
    width = source.shape[0]
    count = width // step

    def piece(i):
        here = pl.ds(i * step, step)
        return pltpu.make_async_copy(source.at[here, :], weights.at[slot, here, :], sems.at[i])

    for i in range(count):
        piece(i).start()
    for i in range(count):
        piece(i).wait()
        rows = slice(i * step, (i + 1) * step)

        def turn(j, _):
            across = pl.ds(pl.multiple_of(j * step, step), step)
            turned[slot, across, rows] = weights[slot, rows, across].T

        lax.fori_loop(0, count, turn, None)


def place(whole, buffers):
    step = 256
    return pl.pallas_call(
        functools.partial(place_kernel, step),
        out_shape=[pltpu.VMEM((2,) + whole.shape, BF16)] * 2,
        in_specs=[HBM] + [VMEM] * len(buffers),
        out_specs=[VMEM] * 2,
        input_output_aliases={1 + i: i for i in range(len(buffers))},
        scratch_shapes=[pltpu.SemaphoreType.DMA((whole.shape[0] // step,))],
        compiler_params=pltpu.CompilerParams(vmem_limit_bytes=LIMIT),
        name="place_weight",
    )(whole, *[held(b) for b in buffers])


def normalize(acts):
    values = acts.astype(F32)
    center = values - jnp.mean(values, axis=-1, keepdims=True)
    variance = jnp.mean(center * center, axis=-1, keepdims=True)
    inverse = 1.0 / jnp.sqrt(variance + 1e-05)
    return center * inverse, inverse


def project(x, gain, weight_ref, into, scaled):
    normed, _ = normalize(x)
    scaled[...] = (normed * gain).astype(BF16)
    width = weight_ref.shape[1]
    tile = width // 2
    for i in range(0, width, tile):
        here = slice(i, i + tile)
        product = jnp.dot(scaled[...], weight_ref[:, here], preferred_element_type=F32)
        into[:, here] = (x[:, here].astype(F32) + product).astype(BF16)


def pull_back(grad, x, gain, turned_ref, into, total, back):
    width = turned_ref.shape[1]
    tile = width // 2
    for i in range(0, width, tile):
        here = slice(i, i + tile)
        back[:, here] = jnp.dot(grad, turned_ref[:, here], preferred_element_type=F32)
    normed, inverse = normalize(x)
    back_proj = back[...]
    scaled = back_proj * gain
    mean_one = jnp.mean(scaled, axis=-1, keepdims=True)
    mean_two = jnp.mean(scaled * normed, axis=-1, keepdims=True)
    norm_grad = inverse * (scaled - mean_one - normed * mean_two)
    into[...] = (grad.astype(F32) + norm_grad).astype(BF16)
    total[...] = total[...] + jnp.sum(back_proj * normed, axis=0, keepdims=True)


def forward_kernel(tick, stages, state, fresh, received, gains, weights, _, *rest):
    sent, stash, scaled = rest[-3:]
    stage, core = state[0], state[1]
    part = tick - stage

    @pl.when((part >= 0) & (part < stash.shape[0]) & (stage < stages - 1))
    def _():
        x = jnp.where(stage == 0, fresh[...], received[...])
        stash[part, 0] = x
        project(x, gains[0:1, :], weights.at[core], stash.at[part, 1], scaled)
        project(stash[part, 1], gains[1:2, :], weights.at[1 - core], sent, scaled)


def forward(tick, stages, parts, state, fresh, received, gains, weights, turned, stash):
    operands = [state, fresh, received, gains, held(weights), held(turned)] + [held(b) for b in stash]
    return pl.pallas_call(
        functools.partial(forward_kernel, tick, stages),
        out_shape=[
            jax.ShapeDtypeStruct(fresh.shape, BF16),
            pltpu.VMEM((parts, 2) + fresh.shape, BF16),
        ],
        in_specs=[SMEM] + [VMEM] * (len(operands) - 1),
        out_specs=[VMEM] * 2,
        input_output_aliases={6: 1} if stash else {},
        scratch_shapes=[pltpu.VMEM(fresh.shape, BF16)],
        compiler_params=pltpu.CompilerParams(vmem_limit_bytes=LIMIT),
        name="forward",
    )(*operands)


def turn_kernel(part, stages, state, fresh, received, gains, weights, turned, *rest):
    sent, collected, totals, scaled, middle, back = rest[-6:]
    stage, core = state[0], state[1]
    if part == 0:
        totals[...] = jnp.zeros_like(totals)

    @pl.when(stage == stages - 1)
    def _():
        x = received[...]
        project(x, gains[0:1, :], weights.at[core], middle, scaled)
        pull_back(fresh[...], middle[...], gains[1:2, :], turned.at[1 - core], collected.at[part, 1], totals.at[1], back)
        pull_back(collected[part, 1], x, gains[0:1, :], turned.at[core], sent, totals.at[0], back)
        collected[part, 0] = sent[...]


def backward_kernel(tick, stages, state, received, leaving, stash, gains, turned, _, __, sent, collected, totals, back):
    stage, core = state[0], state[1]
    part = tick - (2 * stages - 2 - stage)
    active = (part >= 0) & (part < stash.shape[0]) & (stage < stages - 1)

    @pl.when(active)
    def _():
        pull_back(received[...], stash[part, 1], gains[1:2, :], turned.at[1 - core], collected.at[part, 1], totals.at[1], back)
        pull_back(collected[part, 1], stash[part, 0], gains[0:1, :], turned.at[core], sent, totals.at[0], back)
        collected[part, 0] = sent[...]

    @pl.when(stage == stages - 1)
    def _():
        sent[...] = leaving[...]


def backward(kernel, parts, operands, kept, scratch, name):
    rows, width = operands[1].shape
    count = len(operands)
    return pl.pallas_call(
        kernel,
        out_shape=[
            jax.ShapeDtypeStruct((rows, width), BF16),
            pltpu.VMEM((parts, 2, rows, width), BF16),
            pltpu.VMEM((2, 1, width), F32),
        ],
        in_specs=[SMEM] + [VMEM] * (count + len(kept) - 1),
        out_specs=[VMEM] * 3,
        input_output_aliases={count + i: 1 + i for i in range(len(kept))},
        scratch_shapes=scratch + [pltpu.VMEM((rows, width), F32)],
        compiler_params=pltpu.CompilerParams(vmem_limit_bytes=LIMIT),
        name=name,
    )(*operands, *[held(b) for b in kept])


def per_device(inputs, cotangent, weight, gain, momentum, prev_grads):
    sections = lax.axis_size("section")
    section = lax.axis_index("section")
    stages = sections // 2
    stage, core = section // 2, lax.rem(section, 2)
    batches, rows, width = inputs.shape
    parts = batches // 2
    siblings = [(i, i ^ 1) for i in range(sections)]

    def swap(array):
        return lax.ppermute(array, "section", siblings)

    def ordered(own, other, axis):
        return jnp.where(
            core == 0, jnp.concatenate([own, other], axis), jnp.concatenate([other, own], axis)
        )

    whole = lax.all_gather(weight[0], "dp", axis=0, tiled=True)

    bucket = prev_grads[0, 0].astype(BF16)
    pieces = lax.all_to_all(bucket, "dp", 0, 0, tiled=True).astype(F32)
    summed = jnp.sum(pieces, axis=0, keepdims=True)
    new_momentum = 0.9 * momentum + (summed / lax.axis_size("dp"))[None]

    gains = ordered(gain, swap(gain), 0)
    state = jnp.stack([stage, core]).astype(jnp.int32)
    fresh = lax.dynamic_slice_in_dim(inputs, core * parts, parts, 0)
    target = lax.dynamic_slice_in_dim(cotangent, core * parts, parts, 0)
    fresh = [fresh[m] for m in range(parts)]
    target = [target[m] for m in range(parts)]
    whole, new_momentum, gains, state, fresh, target = lax.optimization_barrier(
        (whole, new_momentum, gains, state, fresh, target)
    )
    received = fresh[0]
    incoming = target[0]
    weights, turned = place(whole, [])
    weights, turned = place(swap(whole), [weights, turned])

    def hops(tick, ahead):
        pairs = []
        for k in range(stages):
            to = k + 1 if ahead else k - 1
            part = tick - k if ahead else tick - (2 * stages - 2 - k)
            if 0 <= to < stages and 0 <= part < parts:
                pairs += [(2 * k + c, 2 * to + c) for c in range(2)]
        return pairs

    stash, kept = [], []
    for tick in range(2 * stages - 2 + parts):
        arrived, returned = received, incoming
        if tick < stages + parts - 2:
            sent, *stash = forward(
                tick, stages, parts, state, fresh[min(tick, parts - 1)], arrived, gains, weights, turned, stash
            )
            received = lax.ppermute(sent, "section", hops(tick, True))
        leaving = incoming
        m = tick - (stages - 1)
        if 0 <= m < parts:
            leaving, *kept = backward(
                functools.partial(turn_kernel, m, stages),
                parts,
                [state, target[m], arrived, gains, held(weights), held(turned)],
                kept,
                [pltpu.VMEM((rows, width), BF16)] * 2,
                "turn",
            )
        if tick >= stages:
            leaving, *kept = backward(
                functools.partial(backward_kernel, tick, stages),
                parts,
                [state, returned, leaving, held(stash[0]), gains, held(turned)],
                kept,
                [],
                "backward",
            )
        pairs = hops(tick, False)
        if pairs:
            incoming = lax.ppermute(leaving, "section", pairs)
    collected, totals = kept

    own = lax.dynamic_index_in_dim(collected, core, 1, keepdims=False)
    other = lax.dynamic_index_in_dim(collected, 1 - core, 1, keepdims=False)
    input_grads = ordered(own, swap(other), 0)[None]
    own_total = lax.dynamic_index_in_dim(totals, core, 0, keepdims=False)
    other_total = lax.dynamic_index_in_dim(totals, 1 - core, 0, keepdims=False)
    gain_grads = (own_total + swap(other_total))[None]
    return input_grads, gain_grads, new_momentum


def solution(mesh):
    in_specs = (
        P(None, "dp", None),
        P(None, "dp", None),
        P("section", "dp", None),
        P("section", None),
        P("section", "dp", None),
        P("section", "dp", None, None),
    )
    out_specs = (P("section", None, "dp", None), P("section", "dp", None), P("section", "dp", None))
    return jax.shard_map(per_device, mesh=mesh, in_specs=in_specs, out_specs=out_specs, check_vma=False)
```

```python
import functools

import jax
import jax.numpy as jnp
from jax import lax
from jax.experimental import pallas as pl
from jax.experimental.pallas import tpu as pltpu
from jax.sharding import PartitionSpec as P

VMEM = pl.BlockSpec(memory_space=pltpu.VMEM)
SMEM = pl.BlockSpec(memory_space=pltpu.SMEM)
HBM = pl.BlockSpec(memory_space=pltpu.HBM)
BF16 = jnp.bfloat16
F32 = jnp.float32
LIMIT = 2 << 20


def held(array):
    return pltpu.with_memory_space_constraint(array, pltpu.VMEM)


def assemble_kernel(*refs):
    *pieces, out, stage, arrived, left = refs
    count = len(pieces) // 2
    copies = []
    for i in range(2):
        at = 0
        for piece in pieces[i * count : (i + 1) * count]:
            rows, columns = piece.shape
            here = (pl.ds(at, rows), pl.ds(i * columns, columns))
            n = len(copies)
            copies.append(
                (
                    pltpu.make_async_copy(piece, stage.at[here], arrived.at[n]),
                    pltpu.make_async_copy(stage.at[here], out.at[here], left.at[n]),
                )
            )
            at += rows
    for into, _ in copies:
        into.start()
    for into, onward in copies:
        into.wait()
        onward.start()
    for _, onward in copies:
        onward.wait()


def assemble(lefts, rights):
    pieces = [pltpu.with_memory_space_constraint(piece, pltpu.HBM) for piece in lefts + rights]
    shape = (sum(piece.shape[0] for piece in lefts), 2 * lefts[0].shape[1])
    return pl.pallas_call(
        assemble_kernel,
        out_shape=pltpu.HBM(shape, BF16),
        in_specs=[HBM] * len(pieces),
        out_specs=HBM,
        scratch_shapes=[pltpu.VMEM(shape, BF16)] + [pltpu.SemaphoreType.DMA((len(pieces),))] * 2,
        compiler_params=pltpu.CompilerParams(vmem_limit_bytes=16 << 20),
        name="assemble",
    )(*pieces)


def place_kernel(layouts, state, *rest):
    weights, sems = rest[-3], rest[-1]
    row, col = state[2], state[3]
    height = weights.shape[1] // 32
    copies = []
    for source, (slot, shifts) in zip(rest, layouts):
        for i, shift in enumerate(shifts):
            for j, across in enumerate((0, -1, 1, -2)):
                replica = lax.rem(row + across + 4, 4) * 8 + lax.rem(col + shift + 8, 8)
                into = weights.at[slot, pl.ds(pl.multiple_of(replica * height, 16), height), :]
                at = (i * 4 + j) * height
                copies.append(pltpu.make_async_copy(source.at[at : at + height, :], into, sems.at[len(copies)]))
    for copy in copies:
        copy.start()
    for copy in copies:
        copy.wait()


def place(state, layouts, pieces, buffers):
    width = pieces[0].shape[1]
    pieces = [pltpu.with_memory_space_constraint(piece, pltpu.HBM) for piece in pieces]
    copies = 4 * sum(len(shifts) for _, shifts in layouts)
    return pl.pallas_call(
        functools.partial(place_kernel, layouts),
        out_shape=[pltpu.VMEM((2, width, width), BF16)] * 2,
        in_specs=[SMEM] + [HBM] * len(pieces) + [VMEM] * len(buffers),
        out_specs=[VMEM] * 2,
        input_output_aliases={1 + len(pieces) + i: i for i in range(len(buffers))},
        scratch_shapes=[pltpu.SemaphoreType.DMA((copies,))],
        compiler_params=pltpu.CompilerParams(vmem_limit_bytes=LIMIT),
        name="place_weight",
    )(state, *pieces, *[held(b) for b in buffers])


def pack_kernel(collected, totals, packed):
    parts, rows = collected.shape[1:3]
    for m in range(parts):
        packed[m * rows : (m + 1) * rows, :] = collected[1, m]
    total = totals[1]
    head = total.astype(BF16).astype(F32)
    row = lax.broadcasted_iota(jnp.int32, (16, total.shape[1]), 0)
    tail = jnp.where(row == 0, head, jnp.where(row == 1, total - head, 0.0))
    packed[parts * rows :, :] = tail.astype(BF16)


def pack(collected, totals):
    _, parts, rows, width = collected.shape
    return pl.pallas_call(
        pack_kernel,
        out_shape=jax.ShapeDtypeStruct((parts * rows + 16, width), BF16),
        in_specs=[VMEM] * 2,
        out_specs=VMEM,
        compiler_params=pltpu.CompilerParams(vmem_limit_bytes=LIMIT),
        name="pack",
    )(held(collected), held(totals))


def transpose_kernel(early, state, weights, _, turned):
    step = 256
    count = weights.shape[1] // step

    @pl.when((state[0] <= 1) == early)
    def _():
        def turn(i, _):
            rows = pl.ds(pl.multiple_of(i * step, step), step)
            for slot in range(2):
                for j in range(0, count * step, step):
                    turned[slot, j : j + step, rows] = weights[slot, rows, j : j + step].T

        lax.fori_loop(0, count, turn, None)


def transpose(early, state, weights, turned):
    return pl.pallas_call(
        functools.partial(transpose_kernel, early),
        out_shape=pltpu.VMEM(weights.shape, BF16),
        in_specs=[SMEM] + [VMEM] * 2,
        out_specs=VMEM,
        input_output_aliases={2: 0},
        compiler_params=pltpu.CompilerParams(vmem_limit_bytes=LIMIT),
        name="transpose_weight",
    )(state, held(weights), held(turned))


def normalize(acts):
    values = acts.astype(F32)
    center = values - jnp.mean(values, axis=-1, keepdims=True)
    variance = jnp.mean(center * center, axis=-1, keepdims=True)
    inverse = 1.0 / jnp.sqrt(variance + 1e-05)
    return center * inverse, inverse


def project(x, gain, weight_ref, into, scaled):
    normed, _ = normalize(x)
    scaled[...] = (normed * gain).astype(BF16)
    width = weight_ref.shape[1]
    tile = width // 2
    for i in range(0, width, tile):
        here = slice(i, i + tile)
        product = jnp.dot(scaled[...], weight_ref[:, here], preferred_element_type=F32)
        into[:, here] = (x[:, here].astype(F32) + product).astype(BF16)


def pull_back(grad, x, gain, turned_ref, into, total, back):
    width = turned_ref.shape[1]
    tile = width // 2
    for i in range(0, width, tile):
        here = slice(i, i + tile)
        back[:, here] = jnp.dot(grad, turned_ref[:, here], preferred_element_type=F32)
    normed, inverse = normalize(x)
    back_proj = back[...]
    scaled = back_proj * gain
    mean_one = jnp.mean(scaled, axis=-1, keepdims=True)
    mean_two = jnp.mean(scaled * normed, axis=-1, keepdims=True)
    norm_grad = inverse * (scaled - mean_one - normed * mean_two)
    into[...] = (grad.astype(F32) + norm_grad).astype(BF16)
    total[...] = total[...] + jnp.sum(back_proj * normed, axis=0, keepdims=True)


def forward_kernel(k, part, state, arrived, gains, weights, *rest):
    sent, stash, scaled = rest[-3:]
    core = state[1]

    @pl.when(state[0] == k)
    def _():
        x = arrived[...]
        stash[part, 0] = x
        project(x, gains[0:1, :], weights.at[core], stash.at[part, 1], scaled)
        project(stash[part, 1], gains[1:2, :], weights.at[1 - core], sent, scaled)


def forward(k, part, parts, state, arrived, gains, weights, turned, stash):
    operands = [state, arrived, gains, held(weights), held(turned)] + [held(b) for b in stash]
    return pl.pallas_call(
        functools.partial(forward_kernel, k, part),
        out_shape=[
            jax.ShapeDtypeStruct(arrived.shape, BF16),
            pltpu.VMEM((parts, 2) + arrived.shape, BF16),
        ],
        in_specs=[SMEM] + [VMEM] * (len(operands) - 1),
        out_specs=[VMEM] * 2,
        input_output_aliases={5: 1} if stash else {},
        scratch_shapes=[pltpu.VMEM(arrived.shape, BF16)],
        compiler_params=pltpu.CompilerParams(vmem_limit_bytes=LIMIT),
        name="forward",
    )(*operands)


def turn_kernel(part, stages, state, fresh, received, gains, weights, turned, *rest):
    sent, collected, totals, scaled, middle, back = rest[-6:]
    stage, core = state[0], state[1]
    if part == 0:
        totals[...] = jnp.zeros_like(totals)

    @pl.when(stage == stages - 1)
    def _():
        x = received[...]
        project(x, gains[0:1, :], weights.at[core], middle, scaled)
        pull_back(
            fresh[...], middle[...], gains[1:2, :], turned.at[1 - core], collected.at[1 - core, part], totals.at[1 - core], back
        )
        pull_back(collected[1 - core, part], x, gains[0:1, :], turned.at[core], sent, totals.at[core], back)
        collected[core, part] = sent[...]


def backward_kernel(k, part, state, received, stash, gains, turned, *rest):
    sent, collected, totals, back = rest[-4:]
    core = state[1]

    @pl.when(state[0] == k)
    def _():
        pull_back(
            received[...], stash[part, 1], gains[1:2, :], turned.at[1 - core], collected.at[1 - core, part], totals.at[1 - core], back
        )
        pull_back(collected[1 - core, part], stash[part, 0], gains[0:1, :], turned.at[core], sent, totals.at[core], back)
        collected[core, part] = sent[...]


def backward(kernel, parts, operands, kept, scratch, name):
    rows, width = operands[1].shape
    count = len(operands)
    return pl.pallas_call(
        kernel,
        out_shape=[
            jax.ShapeDtypeStruct((rows, width), BF16),
            pltpu.VMEM((2, parts, rows, width), BF16),
            pltpu.VMEM((2, 1, width), F32),
        ],
        in_specs=[SMEM] + [VMEM] * (count + len(kept) - 1),
        out_specs=[VMEM] * 3,
        input_output_aliases={count + i: 1 + i for i in range(len(kept))},
        scratch_shapes=scratch + [pltpu.VMEM((rows, width), F32)],
        compiler_params=pltpu.CompilerParams(vmem_limit_bytes=LIMIT),
        name=name,
    )(*operands, *[held(b) for b in kept])


def per_device(inputs, cotangent, weight, gain, momentum, prev_grads):
    sections = lax.axis_size("section")
    section = lax.axis_index("section")
    stages = sections // 2
    stage, core = section // 2, lax.rem(section, 2)
    batches, rows, width = inputs.shape
    parts = batches // 2
    siblings = [(i, i ^ 1) for i in range(sections)]

    def swap(array):
        return lax.ppermute(array, "section", siblings)

    def ordered(own, other):
        return jnp.where(core == 0, jnp.concatenate([own, other], 0), jnp.concatenate([other, own], 0))

    def unpacked(block):
        return block[0:1].astype(F32) + block[1:2].astype(F32)

    def over(array, rows, columns):
        pairs = [
            (y * 8 + z, ((y + rows) % 4) * 8 + (z + columns) % 8) for y in range(4) for z in range(8)
        ]
        return lax.ppermute(array, "dp", pairs)

    def first_block(shard):
        above, below = over(shard, 1, 0), over(shard, -1, 0)
        return jnp.concatenate([shard, above, below, over(above, 1, 0)], 0)

    bucket = prev_grads[0, 0].astype(BF16)
    pieces = lax.all_to_all(bucket, "dp", 0, 0, tiled=True).astype(F32)
    summed = jnp.sum(pieces, axis=0, keepdims=True)
    new_momentum = 0.9 * momentum + (summed / lax.axis_size("dp"))[None]

    half = width // 2
    shards = [weight[0, :, :half], weight[0, :, half:]]
    shards[1], new_momentum = lax.optimization_barrier((shards[1], new_momentum))
    blocks = [first_block(shard) for shard in shards]
    rings = [[(block, block)] for block in blocks]
    for step in range(3):
        for ring in rings:
            right, left = ring[-1]
            ring.append(lax.optimization_barrier((over(right, 0, 1), over(left, 0, -1))))
    ends = [over(rings[0][3][0], 0, 1), over(rings[1][3][1], 0, -1)]
    inner = [[ring[0][0], *ring[1], *ring[2]] for ring in rings]
    inner, rings[0][3], rings[1][3] = lax.optimization_barrier((inner, rings[0][3], rings[1][3]))
    inner = assemble(*inner)
    inner_other = swap(inner)

    outer = assemble(*[[*ring[3], end] for ring, end in zip(rings, ends)])
    outer_other = swap(outer)

    gains = ordered(gain, swap(gain))
    replica = lax.axis_index("dp")
    state = jnp.stack([stage, core, replica // 8, lax.rem(replica, 8)]).astype(jnp.int32)
    fresh = lax.dynamic_slice_in_dim(inputs, core * parts, parts, 0)
    target = lax.dynamic_slice_in_dim(cotangent, core * parts, parts, 0)
    fresh = [fresh[m] for m in range(parts)]
    target = [target[m] for m in range(parts)]
    gains, state, fresh, target, outer = lax.optimization_barrier((gains, state, fresh, target, outer))
    near, far = (0, -1, 1, -2, 2), (-3, 3, 4)
    buffers = place(state, ((0, near), (0, far), (1, near)), [inner, outer, inner_other], [])
    weights, turned = place(state, ((1, far),), [outer_other], buffers)
    turned = transpose(False, state, weights, turned)

    def hop(array, k, to, after):
        if after is not None:
            array, after = lax.optimization_barrier((array, after))
        return lax.ppermute(array, "section", [(2 * k + c, 2 * to + c) for c in range(2)])

    arrived = fresh
    stash, kept = [], []
    for k in range(stages - 1):
        landed = []
        for m in range(parts):
            sent, *stash = forward(k, m, parts, state, arrived[m], gains, weights, turned, stash)
            landed.append(hop(sent, k, k + 1, landed[-1] if landed else None))
        arrived = landed
        if k == 3:
            turned = transpose(True, state, weights, turned)
    for k in range(stages - 1, -1, -1):
        landed = []
        for m in range(parts):
            if k == stages - 1:
                kernel, scratch = functools.partial(turn_kernel, m, stages), [pltpu.VMEM((rows, width), BF16)] * 2
                operands = [state, target[m], arrived[m], gains, held(weights), held(turned)]
            else:
                kernel, scratch = functools.partial(backward_kernel, k, m), []
                operands = [state, arrived[m], held(stash[0]), gains, held(turned), held(weights)]
            leaving, *kept = backward(kernel, parts, operands, kept, scratch, "turn" if scratch else "backward")
            if k > 0:
                landed.append(hop(leaving, k, k - 1, landed[-1] if landed else None))
        arrived = landed
    collected, totals = kept

    other = swap(pack(collected, totals))
    input_grads = ordered(collected[0], other[: parts * rows].reshape(parts, rows, width))[None]
    gain_grads = (totals[0] + unpacked(other[parts * rows :]))[None]

    return input_grads, gain_grads, new_momentum


def solution(mesh):
    in_specs = (
        P(None, "dp", None),
        P(None, "dp", None),
        P("section", "dp", None),
        P("section", None),
        P("section", "dp", None),
        P("section", "dp", None, None),
    )
    out_specs = (P("section", None, "dp", None), P("section", "dp", None), P("section", "dp", None))
    return jax.shard_map(per_device, mesh=mesh, in_specs=in_specs, out_specs=out_specs, check_vma=False)
```

```python
import functools

import jax
import jax.numpy as jnp
from jax import lax
from jax.experimental import pallas as pl
from jax.experimental.pallas import tpu as pltpu
from jax.sharding import PartitionSpec as P

VMEM = pl.BlockSpec(memory_space=pltpu.VMEM)
SMEM = pl.BlockSpec(memory_space=pltpu.SMEM)
HBM = pl.BlockSpec(memory_space=pltpu.HBM)
BF16 = jnp.bfloat16
F32 = jnp.float32
LIMIT = 2 << 20


def held(array):
    return pltpu.with_memory_space_constraint(array, pltpu.VMEM)


def assemble_kernel(*refs):
    *pieces, out, stage, arrived, left = refs
    count = len(pieces) // 2
    copies = []
    for i in range(2):
        at = 0
        for piece in pieces[i * count : (i + 1) * count]:
            rows, columns = piece.shape
            here = (pl.ds(at, rows), pl.ds(i * columns, columns))
            n = len(copies)
            copies.append(
                (
                    pltpu.make_async_copy(piece, stage.at[here], arrived.at[n]),
                    pltpu.make_async_copy(stage.at[here], out.at[here], left.at[n]),
                )
            )
            at += rows
    for into, _ in copies:
        into.start()
    for into, onward in copies:
        into.wait()
        onward.start()
    for _, onward in copies:
        onward.wait()


def assemble(lefts, rights):
    pieces = [pltpu.with_memory_space_constraint(piece, pltpu.HBM) for piece in lefts + rights]
    shape = (sum(piece.shape[0] for piece in lefts), 2 * lefts[0].shape[1])
    return pl.pallas_call(
        assemble_kernel,
        out_shape=pltpu.HBM(shape, BF16),
        in_specs=[HBM] * len(pieces),
        out_specs=HBM,
        scratch_shapes=[pltpu.VMEM(shape, BF16)] + [pltpu.SemaphoreType.DMA((len(pieces),))] * 2,
        compiler_params=pltpu.CompilerParams(vmem_limit_bytes=16 << 20),
        name="assemble",
    )(*pieces)


def place_kernel(layouts, state, *rest):
    weights, sems = rest[-3], rest[-1]
    row, col = state[2], state[3]
    height = weights.shape[1] // 32
    copies = []
    for source, (slot, shifts) in zip(rest, layouts):
        for i, shift in enumerate(shifts):
            for j, across in enumerate((0, -1, 1, -2)):
                replica = lax.rem(row + across + 4, 4) * 8 + lax.rem(col + shift + 8, 8)
                into = weights.at[slot, pl.ds(pl.multiple_of(replica * height, 16), height), :]
                at = (i * 4 + j) * height
                copies.append(pltpu.make_async_copy(source.at[at : at + height, :], into, sems.at[len(copies)]))
    for copy in copies:
        copy.start()
    for copy in copies:
        copy.wait()


def place(state, layouts, pieces, buffers):
    width = pieces[0].shape[1]
    pieces = [pltpu.with_memory_space_constraint(piece, pltpu.HBM) for piece in pieces]
    copies = 4 * sum(len(shifts) for _, shifts in layouts)
    return pl.pallas_call(
        functools.partial(place_kernel, layouts),
        out_shape=[pltpu.VMEM((2, width, width), BF16)] * 2,
        in_specs=[SMEM] + [HBM] * len(pieces) + [VMEM] * len(buffers),
        out_specs=[VMEM] * 2,
        input_output_aliases={1 + len(pieces) + i: i for i in range(len(buffers))},
        scratch_shapes=[pltpu.SemaphoreType.DMA((copies,))],
        compiler_params=pltpu.CompilerParams(vmem_limit_bytes=LIMIT),
        name="place_weight",
    )(state, *pieces, *[held(b) for b in buffers])


def pack_kernel(collected, totals, packed):
    parts, rows = collected.shape[1:3]
    for m in range(parts):
        packed[m * rows : (m + 1) * rows, :] = collected[1, m]
    total = totals[1]
    head = total.astype(BF16).astype(F32)
    row = lax.broadcasted_iota(jnp.int32, (16, total.shape[1]), 0)
    tail = jnp.where(row == 0, head, jnp.where(row == 1, total - head, 0.0))
    packed[parts * rows :, :] = tail.astype(BF16)


def pack(collected, totals):
    _, parts, rows, width = collected.shape
    return pl.pallas_call(
        pack_kernel,
        out_shape=jax.ShapeDtypeStruct((parts * rows + 16, width), BF16),
        in_specs=[VMEM] * 2,
        out_specs=VMEM,
        compiler_params=pltpu.CompilerParams(vmem_limit_bytes=LIMIT),
        name="pack",
    )(held(collected), held(totals))


def transpose_kernel(early, state, weights, _, turned):
    step = 256
    count = weights.shape[1] // step

    @pl.when((state[0] <= 1) == early)
    def _():
        def turn(i, _):
            rows = pl.ds(pl.multiple_of(i * step, step), step)
            for slot in range(2):
                for j in range(0, count * step, step):
                    turned[slot, j : j + step, rows] = weights[slot, rows, j : j + step].T

        lax.fori_loop(0, count, turn, None)


def transpose(early, state, weights, turned):
    return pl.pallas_call(
        functools.partial(transpose_kernel, early),
        out_shape=pltpu.VMEM(weights.shape, BF16),
        in_specs=[SMEM] + [VMEM] * 2,
        out_specs=VMEM,
        input_output_aliases={2: 0},
        compiler_params=pltpu.CompilerParams(vmem_limit_bytes=LIMIT),
        name="transpose_weight",
    )(state, held(weights), held(turned))


def normalize(acts):
    values = acts.astype(F32)
    center = values - jnp.mean(values, axis=-1, keepdims=True)
    variance = jnp.mean(center * center, axis=-1, keepdims=True)
    inverse = 1.0 / jnp.sqrt(variance + 1e-05)
    return center * inverse, inverse


def project(x, gain, weight_ref, into, scaled):
    normed, _ = normalize(x)
    scaled[...] = (normed * gain).astype(BF16)
    width = weight_ref.shape[1]
    tile = width // 2
    for i in range(0, width, tile):
        here = slice(i, i + tile)
        product = jnp.dot(scaled[...], weight_ref[:, here], preferred_element_type=F32)
        into[:, here] = (x[:, here].astype(F32) + product).astype(BF16)


def pull_back(grad, x, gain, turned_ref, into, total, back):
    width = turned_ref.shape[1]
    tile = width // 2
    for i in range(0, width, tile):
        here = slice(i, i + tile)
        back[:, here] = jnp.dot(grad, turned_ref[:, here], preferred_element_type=F32)
    normed, inverse = normalize(x)
    back_proj = back[...]
    scaled = back_proj * gain
    mean_one = jnp.mean(scaled, axis=-1, keepdims=True)
    mean_two = jnp.mean(scaled * normed, axis=-1, keepdims=True)
    norm_grad = inverse * (scaled - mean_one - normed * mean_two)
    into[...] = (grad.astype(F32) + norm_grad).astype(BF16)
    total[...] = total[...] + jnp.sum(back_proj * normed, axis=0, keepdims=True)


def forward_kernel(k, part, state, arrived, gains, weights, *rest):
    sent, stash, scaled = rest[-3:]
    core = state[1]

    @pl.when(state[0] == k)
    def _():
        x = arrived[...]
        stash[part, 0] = x
        project(x, gains[0:1, :], weights.at[core], stash.at[part, 1], scaled)
        project(stash[part, 1], gains[1:2, :], weights.at[1 - core], sent, scaled)


def forward(k, part, parts, state, arrived, gains, weights, turned, stash):
    operands = [state, arrived, gains, held(weights), held(turned)] + [held(b) for b in stash]
    return pl.pallas_call(
        functools.partial(forward_kernel, k, part),
        out_shape=[
            jax.ShapeDtypeStruct(arrived.shape, BF16),
            pltpu.VMEM((parts, 2) + arrived.shape, BF16),
        ],
        in_specs=[SMEM] + [VMEM] * (len(operands) - 1),
        out_specs=[VMEM] * 2,
        input_output_aliases={5: 1} if stash else {},
        scratch_shapes=[pltpu.VMEM(arrived.shape, BF16)],
        compiler_params=pltpu.CompilerParams(vmem_limit_bytes=LIMIT),
        name="forward",
    )(*operands)


def turn_kernel(part, stages, state, fresh, received, gains, weights, turned, *rest):
    sent, collected, totals, scaled, middle, back = rest[-6:]
    stage, core = state[0], state[1]
    if part == 0:
        totals[...] = jnp.zeros_like(totals)

    @pl.when(stage == stages - 1)
    def _():
        x = received[...]
        project(x, gains[0:1, :], weights.at[core], middle, scaled)
        pull_back(
            fresh[...], middle[...], gains[1:2, :], turned.at[1 - core], collected.at[1 - core, part], totals.at[1 - core], back
        )
        pull_back(collected[1 - core, part], x, gains[0:1, :], turned.at[core], sent, totals.at[core], back)
        collected[core, part] = sent[...]


def backward_kernel(k, part, state, received, stash, gains, turned, *rest):
    sent, collected, totals, back = rest[-4:]
    core = state[1]

    @pl.when(state[0] == k)
    def _():
        pull_back(
            received[...], stash[part, 1], gains[1:2, :], turned.at[1 - core], collected.at[1 - core, part], totals.at[1 - core], back
        )
        pull_back(collected[1 - core, part], stash[part, 0], gains[0:1, :], turned.at[core], sent, totals.at[core], back)
        collected[core, part] = sent[...]


def backward(kernel, parts, operands, kept, scratch, name):
    rows, width = operands[1].shape
    count = len(operands)
    return pl.pallas_call(
        kernel,
        out_shape=[
            jax.ShapeDtypeStruct((rows, width), BF16),
            pltpu.VMEM((2, parts, rows, width), BF16),
            pltpu.VMEM((2, 1, width), F32),
        ],
        in_specs=[SMEM] + [VMEM] * (count + len(kept) - 1),
        out_specs=[VMEM] * 3,
        input_output_aliases={count + i: 1 + i for i in range(len(kept))},
        scratch_shapes=scratch + [pltpu.VMEM((rows, width), F32)],
        compiler_params=pltpu.CompilerParams(vmem_limit_bytes=LIMIT),
        name=name,
    )(*operands, *[held(b) for b in kept])


def per_device(inputs, cotangent, weight, gain, momentum, prev_grads):
    sections = lax.axis_size("section")
    section = lax.axis_index("section")
    stages = sections // 2
    stage, core = section // 2, lax.rem(section, 2)
    batches, rows, width = inputs.shape
    parts = batches // 2
    siblings = [(i, i ^ 1) for i in range(sections)]

    def swap(array):
        return lax.ppermute(array, "section", siblings)

    def ordered(own, other):
        return jnp.where(core == 0, jnp.concatenate([own, other], 0), jnp.concatenate([other, own], 0))

    def unpacked(block):
        return block[0:1].astype(F32) + block[1:2].astype(F32)

    def over(array, rows, columns):
        pairs = [
            (y * 8 + z, ((y + rows) % 4) * 8 + (z + columns) % 8) for y in range(4) for z in range(8)
        ]
        return lax.ppermute(array, "dp", pairs)

    def first_block(shard):
        above, below = over(shard, 1, 0), over(shard, -1, 0)
        return jnp.concatenate([shard, above, below, over(above, 1, 0)], 0)

    bucket = prev_grads[0, 0].astype(BF16)
    pieces = lax.all_to_all(bucket, "dp", 0, 0, tiled=True).astype(F32)
    summed = jnp.sum(pieces, axis=0, keepdims=True)
    new_momentum = 0.9 * momentum + (summed / lax.axis_size("dp"))[None]

    half = width // 2
    shards = [weight[0, :, :half], weight[0, :, half:]]
    gains = ordered(gain, swap(gain))
    shards[1], new_momentum, gains = lax.optimization_barrier((shards[1], new_momentum, gains))
    blocks = [first_block(shard) for shard in shards]
    rings = [[(block, block)] for block in blocks]
    for step in range(3):
        for ring in rings:
            right, left = ring[-1]
            ring.append(lax.optimization_barrier((over(right, 0, 1), over(left, 0, -1))))
    ends = [over(rings[0][3][0], 0, 1), over(rings[1][3][1], 0, -1)]
    inner = [[ring[0][0], *ring[1], *ring[2]] for ring in rings]
    inner, rings[0][3], rings[1][3] = lax.optimization_barrier((inner, rings[0][3], rings[1][3]))
    inner = assemble(*inner)
    inner_other = swap(inner)

    outer = assemble(*[[*ring[3], end] for ring, end in zip(rings, ends)])
    outer_other = swap(outer)

    replica = lax.axis_index("dp")
    state = jnp.stack([stage, core, replica // 8, lax.rem(replica, 8)]).astype(jnp.int32)
    fresh = lax.dynamic_slice_in_dim(inputs, core * parts, parts, 0)
    target = lax.dynamic_slice_in_dim(cotangent, core * parts, parts, 0)
    fresh = [fresh[m] for m in range(parts)]
    target = [target[m] for m in range(parts)]
    gains, state, fresh, target, outer = lax.optimization_barrier((gains, state, fresh, target, outer))
    near, far = (0, -1, 1, -2, 2), (-3, 3, 4)
    buffers = place(state, ((0, near), (0, far), (1, near)), [inner, outer, inner_other], [])
    weights, turned = place(state, ((1, far),), [outer_other], buffers)
    turned = transpose(False, state, weights, turned)

    def hop(array, k, to, after):
        array, _ = lax.optimization_barrier((array, after))
        return lax.ppermute(array, "section", [(2 * k + c, 2 * to + c) for c in range(2)])

    arrived = fresh
    stash, kept = [], []
    path = [(k, k + 1) for k in range(stages - 1)] + [(k, k - 1) for k in range(stages - 1, -1, -1)]
    waiting = None
    for at, (k, to) in enumerate(path):
        landed = []
        for m in range(parts):
            if m == parts - 1 and waiting is not None:
                arrived.append(hop(*waiting, [arrived[m - 1], landed[-1] if landed else leaving]))
                waiting = None
            if to > k:
                leaving, *stash = forward(k, m, parts, state, arrived[m], gains, weights, turned, stash)
            else:
                if k == stages - 1:
                    kernel, scratch = functools.partial(turn_kernel, m, stages), [pltpu.VMEM((rows, width), BF16)] * 2
                    operands = [state, target[m], arrived[m], gains, held(weights), held(turned)]
                else:
                    kernel, scratch = functools.partial(backward_kernel, k, m), []
                    operands = [state, arrived[m], held(stash[0]), gains, held(turned), held(weights)]
                leaving, *kept = backward(kernel, parts, operands, kept, scratch, "turn" if scratch else "backward")
            if to < 0:
                continue
            if m < parts - 1 or to == stages - 1:
                landed.append(hop(leaving, k, to, landed[-1:]))
            else:
                waiting = (leaving, k, to)
        arrived = landed
        if at == 3:
            turned = transpose(True, state, weights, turned)
    collected, totals = kept

    other = swap(pack(collected, totals))
    input_grads = ordered(collected[0], other[: parts * rows].reshape(parts, rows, width))[None]
    gain_grads = (totals[0] + unpacked(other[parts * rows :]))[None]

    return input_grads, gain_grads, new_momentum


def solution(mesh):
    in_specs = (
        P(None, "dp", None),
        P(None, "dp", None),
        P("section", "dp", None),
        P("section", None),
        P("section", "dp", None),
        P("section", "dp", None, None),
    )
    out_specs = (P("section", None, "dp", None), P("section", "dp", None), P("section", "dp", None))
    return jax.shard_map(per_device, mesh=mesh, in_specs=in_specs, out_specs=out_specs, check_vma=False)
```

```python
import functools

import jax
import jax.numpy as jnp
from jax import lax
from jax.experimental import pallas as pl
from jax.experimental.pallas import tpu as pltpu
from jax.sharding import PartitionSpec as P

VMEM = pl.BlockSpec(memory_space=pltpu.VMEM)
SMEM = pl.BlockSpec(memory_space=pltpu.SMEM)
HBM = pl.BlockSpec(memory_space=pltpu.HBM)
BF16 = jnp.bfloat16
F32 = jnp.float32
LIMIT = 2 << 20


def held(array):
    return pltpu.with_memory_space_constraint(array, pltpu.VMEM)


def assemble_kernel(*refs):
    *pieces, out, stage, arrived, left = refs
    count = len(pieces) // 2
    copies = []
    for i in range(2):
        at = 0
        for piece in pieces[i * count : (i + 1) * count]:
            rows, columns = piece.shape
            here = (pl.ds(at, rows), pl.ds(i * columns, columns))
            n = len(copies)
            copies.append(
                (
                    pltpu.make_async_copy(piece, stage.at[here], arrived.at[n]),
                    pltpu.make_async_copy(stage.at[here], out.at[here], left.at[n]),
                )
            )
            at += rows
    for into, _ in copies:
        into.start()
    for into, onward in copies:
        into.wait()
        onward.start()
    for _, onward in copies:
        onward.wait()


def assemble(lefts, rights):
    pieces = [pltpu.with_memory_space_constraint(piece, pltpu.HBM) for piece in lefts + rights]
    shape = (sum(piece.shape[0] for piece in lefts), 2 * lefts[0].shape[1])
    return pl.pallas_call(
        assemble_kernel,
        out_shape=pltpu.HBM(shape, BF16),
        in_specs=[HBM] * len(pieces),
        out_specs=HBM,
        scratch_shapes=[pltpu.VMEM(shape, BF16)] + [pltpu.SemaphoreType.DMA((len(pieces),))] * 2,
        compiler_params=pltpu.CompilerParams(vmem_limit_bytes=16 << 20),
        name="assemble",
    )(*pieces)


def place_kernel(layouts, state, *rest):
    weights, sems = rest[-3], rest[-1]
    row, col = state[2], state[3]
    height = weights.shape[1] // 32
    copies = []
    for source, (slot, shifts) in zip(rest, layouts):
        for i, shift in enumerate(shifts):
            for j, across in enumerate((0, -1, 1, -2)):
                replica = lax.rem(row + across + 4, 4) * 8 + lax.rem(col + shift + 8, 8)
                into = weights.at[slot, pl.ds(pl.multiple_of(replica * height, 16), height), :]
                at = (i * 4 + j) * height
                copies.append(pltpu.make_async_copy(source.at[at : at + height, :], into, sems.at[len(copies)]))
    for copy in copies:
        copy.start()
    for copy in copies:
        copy.wait()


def place(state, layouts, pieces, buffers):
    width = pieces[0].shape[1]
    pieces = [pltpu.with_memory_space_constraint(piece, pltpu.HBM) for piece in pieces]
    copies = 4 * sum(len(shifts) for _, shifts in layouts)
    return pl.pallas_call(
        functools.partial(place_kernel, layouts),
        out_shape=[pltpu.VMEM((2, width, width), BF16)] * 2,
        in_specs=[SMEM] + [HBM] * len(pieces) + [VMEM] * len(buffers),
        out_specs=[VMEM] * 2,
        input_output_aliases={1 + len(pieces) + i: i for i in range(len(buffers))},
        scratch_shapes=[pltpu.SemaphoreType.DMA((copies,))],
        compiler_params=pltpu.CompilerParams(vmem_limit_bytes=LIMIT),
        name="place_weight",
    )(state, *pieces, *[held(b) for b in buffers])


def pack_kernel(collected, totals, packed):
    parts, rows = collected.shape[1:3]
    for m in range(parts):
        packed[m * rows : (m + 1) * rows, :] = collected[1, m]
    total = totals[1]
    head = total.astype(BF16).astype(F32)
    row = lax.broadcasted_iota(jnp.int32, (16, total.shape[1]), 0)
    tail = jnp.where(row == 0, head, jnp.where(row == 1, total - head, 0.0))
    packed[parts * rows :, :] = tail.astype(BF16)


def pack(collected, totals):
    _, parts, rows, width = collected.shape
    return pl.pallas_call(
        pack_kernel,
        out_shape=jax.ShapeDtypeStruct((parts * rows + 16, width), BF16),
        in_specs=[VMEM] * 2,
        out_specs=VMEM,
        compiler_params=pltpu.CompilerParams(vmem_limit_bytes=LIMIT),
        name="pack",
    )(held(collected), held(totals))


def transpose_kernel(early, state, weights, _, turned):
    step = 256
    count = weights.shape[1] // step

    @pl.when((state[0] <= 1) == early)
    def _():
        def turn(i, _):
            rows = pl.ds(pl.multiple_of(i * step, step), step)
            for slot in range(2):
                for j in range(0, count * step, step):
                    turned[slot, j : j + step, rows] = weights[slot, rows, j : j + step].T

        lax.fori_loop(0, count, turn, None)


def transpose(early, state, weights, turned):
    return pl.pallas_call(
        functools.partial(transpose_kernel, early),
        out_shape=pltpu.VMEM(weights.shape, BF16),
        in_specs=[SMEM] + [VMEM] * 2,
        out_specs=VMEM,
        input_output_aliases={2: 0},
        compiler_params=pltpu.CompilerParams(vmem_limit_bytes=LIMIT),
        name="transpose_weight",
    )(state, held(weights), held(turned))


def normalize(acts):
    values = acts.astype(F32)
    center = values - jnp.mean(values, axis=-1, keepdims=True)
    variance = jnp.mean(center * center, axis=-1, keepdims=True)
    inverse = 1.0 / jnp.sqrt(variance + 1e-05)
    return center * inverse, inverse


def project(x, gain, weight_ref, into, scaled):
    normed, _ = normalize(x)
    scaled[...] = (normed * gain).astype(BF16)
    width = weight_ref.shape[1]
    tile = width // 2
    for i in range(0, width, tile):
        here = slice(i, i + tile)
        product = jnp.dot(scaled[...], weight_ref[:, here], preferred_element_type=F32)
        into[:, here] = (x[:, here].astype(F32) + product).astype(BF16)


def pull_back(grad, x, gain, turned_ref, into, total, back):
    width = turned_ref.shape[1]
    tile = width // 2
    for i in range(0, width, tile):
        here = slice(i, i + tile)
        back[:, here] = jnp.dot(grad, turned_ref[:, here], preferred_element_type=F32)
    normed, inverse = normalize(x)
    back_proj = back[...]
    scaled = back_proj * gain
    mean_one = jnp.mean(scaled, axis=-1, keepdims=True)
    mean_two = jnp.mean(scaled * normed, axis=-1, keepdims=True)
    norm_grad = inverse * (scaled - mean_one - normed * mean_two)
    into[...] = (grad.astype(F32) + norm_grad).astype(BF16)
    total[...] = total[...] + jnp.sum(back_proj * normed, axis=0, keepdims=True)


def forward_kernel(k, part, state, arrived, gains, weights, *rest):
    sent, stash, scaled = rest[-3:]
    core = state[1]

    @pl.when(state[0] == k)
    def _():
        x = arrived[...]
        stash[part, 0] = x
        project(x, gains[0:1, :], weights.at[core], stash.at[part, 1], scaled)
        project(stash[part, 1], gains[1:2, :], weights.at[1 - core], sent, scaled)


def forward(k, part, parts, state, arrived, gains, weights, turned, stash):
    operands = [state, arrived, gains, held(weights), held(turned)] + [held(b) for b in stash]
    return pl.pallas_call(
        functools.partial(forward_kernel, k, part),
        out_shape=[
            jax.ShapeDtypeStruct(arrived.shape, BF16),
            pltpu.VMEM((parts, 2) + arrived.shape, BF16),
        ],
        in_specs=[SMEM] + [VMEM] * (len(operands) - 1),
        out_specs=[VMEM] * 2,
        input_output_aliases={5: 1} if stash else {},
        scratch_shapes=[pltpu.VMEM(arrived.shape, BF16)],
        compiler_params=pltpu.CompilerParams(vmem_limit_bytes=LIMIT),
        name="forward",
    )(*operands)


def turn_kernel(part, stages, state, fresh, received, gains, weights, turned, *rest):
    sent, collected, totals, scaled, middle, back = rest[-6:]
    stage, core = state[0], state[1]
    if part == 0:
        totals[...] = jnp.zeros_like(totals)

    @pl.when(stage == stages - 1)
    def _():
        x = received[...]
        project(x, gains[0:1, :], weights.at[core], middle, scaled)
        pull_back(
            fresh[...], middle[...], gains[1:2, :], turned.at[1 - core], collected.at[1 - core, part], totals.at[1 - core], back
        )
        pull_back(collected[1 - core, part], x, gains[0:1, :], turned.at[core], sent, totals.at[core], back)
        collected[core, part] = sent[...]


def backward_kernel(k, part, state, received, stash, gains, turned, *rest):
    sent, collected, totals, back = rest[-4:]
    core = state[1]

    @pl.when(state[0] == k)
    def _():
        pull_back(
            received[...], stash[part, 1], gains[1:2, :], turned.at[1 - core], collected.at[1 - core, part], totals.at[1 - core], back
        )
        pull_back(collected[1 - core, part], stash[part, 0], gains[0:1, :], turned.at[core], sent, totals.at[core], back)
        collected[core, part] = sent[...]


def backward(kernel, parts, operands, kept, scratch, name):
    rows, width = operands[1].shape
    count = len(operands)
    return pl.pallas_call(
        kernel,
        out_shape=[
            jax.ShapeDtypeStruct((rows, width), BF16),
            pltpu.VMEM((2, parts, rows, width), BF16),
            pltpu.VMEM((2, 1, width), F32),
        ],
        in_specs=[SMEM] + [VMEM] * (count + len(kept) - 1),
        out_specs=[VMEM] * 3,
        input_output_aliases={count + i: 1 + i for i in range(len(kept))},
        scratch_shapes=scratch + [pltpu.VMEM((rows, width), F32)],
        compiler_params=pltpu.CompilerParams(vmem_limit_bytes=LIMIT),
        name=name,
    )(*operands, *[held(b) for b in kept])


def per_device(inputs, cotangent, weight, gain, momentum, prev_grads):
    sections = lax.axis_size("section")
    section = lax.axis_index("section")
    stages = sections // 2
    stage, core = section // 2, lax.rem(section, 2)
    batches, rows, width = inputs.shape
    parts = batches // 2
    siblings = [(i, i ^ 1) for i in range(sections)]

    def swap(array):
        return lax.ppermute(array, "section", siblings)

    def ordered(own, other):
        return jnp.where(core == 0, jnp.concatenate([own, other], 0), jnp.concatenate([other, own], 0))

    def unpacked(block):
        return block[0:1].astype(F32) + block[1:2].astype(F32)

    def over(array, rows, columns):
        pairs = [
            (y * 8 + z, ((y + rows) % 4) * 8 + (z + columns) % 8) for y in range(4) for z in range(8)
        ]
        return lax.ppermute(array, "dp", pairs)

    def first_block(shard):
        above, below = over(shard, 1, 0), over(shard, -1, 0)
        return above, jnp.concatenate([shard, above, below, over(above, 1, 0)], 0)

    half = width // 2
    shards = [weight[0, :, :half], weight[0, :, half:]]
    above, block = first_block(shards[0])
    shards[1], _ = lax.optimization_barrier((shards[1], above))
    blocks = [block, first_block(shards[1])[1]]
    rings = [[(block, block)] for block in blocks]
    for step in range(3):
        for ring in rings:
            right, left = ring[-1]
            ring.append(lax.optimization_barrier((over(right, 0, 1), over(left, 0, -1))))
    ends = [over(rings[0][3][0], 0, 1), over(rings[1][3][1], 0, -1)]
    inner = [[ring[0][0], *ring[1], *ring[2]] for ring in rings]
    inner, rings[0][3], rings[1][3] = lax.optimization_barrier((inner, rings[0][3], rings[1][3]))
    inner = assemble(*inner)
    inner_other = swap(inner)
    own_gain, inner = lax.optimization_barrier((gain, inner))
    gains = ordered(gain, swap(own_gain))
    ends, gains = lax.optimization_barrier((ends, gains))

    bucket, inner_other = lax.optimization_barrier((prev_grads[0, 0].astype(BF16), inner_other))
    pieces = lax.all_to_all(bucket, "dp", 0, 0, tiled=True).astype(F32)
    summed = jnp.sum(pieces, axis=0, keepdims=True)
    new_momentum = 0.9 * momentum + (summed / lax.axis_size("dp"))[None]


    ends, new_momentum = lax.optimization_barrier((ends, new_momentum))
    outer = assemble(*[[*ring[3], end] for ring, end in zip(rings, ends)])
    outer_other = swap(outer)

    replica = lax.axis_index("dp")
    state = jnp.stack([stage, core, replica // 8, lax.rem(replica, 8)]).astype(jnp.int32)
    fresh = lax.dynamic_slice_in_dim(inputs, core * parts, parts, 0)
    target = lax.dynamic_slice_in_dim(cotangent, core * parts, parts, 0)
    fresh = [fresh[m] for m in range(parts)]
    target = [target[m] for m in range(parts)]
    gains, state, fresh, target, outer, new_momentum = lax.optimization_barrier(
        (gains, state, fresh, target, outer, new_momentum)
    )
    near, far = (0, -1, 1, -2, 2), (-3, 3, 4)
    buffers = place(state, ((0, near), (0, far), (1, near)), [inner, outer, inner_other], [])
    weights, turned = place(state, ((1, far),), [outer_other], buffers)
    turned = transpose(False, state, weights, turned)

    def hop(array, k, to, after):
        if after is not None:
            array, after = lax.optimization_barrier((array, after))
        return lax.ppermute(array, "section", [(2 * k + c, 2 * to + c) for c in range(2)])

    arrived = fresh
    stash, kept = [], []
    for k in range(stages - 1):
        landed = []
        for m in range(parts):
            sent, *stash = forward(k, m, parts, state, arrived[m], gains, weights, turned, stash)
            landed.append(hop(sent, k, k + 1, landed[-1] if landed else None))
        arrived = landed
        if k == 3:
            turned = transpose(True, state, weights, turned)
    for k in range(stages - 1, -1, -1):
        landed = []
        for m in range(parts):
            if k == stages - 1:
                kernel, scratch = functools.partial(turn_kernel, m, stages), [pltpu.VMEM((rows, width), BF16)] * 2
                operands = [state, target[m], arrived[m], gains, held(weights), held(turned)]
            else:
                kernel, scratch = functools.partial(backward_kernel, k, m), []
                operands = [state, arrived[m], held(stash[0]), gains, held(turned), held(weights)]
            leaving, *kept = backward(kernel, parts, operands, kept, scratch, "turn" if scratch else "backward")
            if k > 0:
                landed.append(hop(leaving, k, k - 1, landed[-1] if landed else None))
        arrived = landed
    collected, totals = kept

    other = swap(pack(collected, totals))
    input_grads = ordered(collected[0], other[: parts * rows].reshape(parts, rows, width))[None]
    gain_grads = (totals[0] + unpacked(other[parts * rows :]))[None]

    return input_grads, gain_grads, new_momentum


def solution(mesh):
    in_specs = (
        P(None, "dp", None),
        P(None, "dp", None),
        P("section", "dp", None),
        P("section", None),
        P("section", "dp", None),
        P("section", "dp", None, None),
    )
    out_specs = (P("section", None, "dp", None), P("section", "dp", None), P("section", "dp", None))
    return jax.shard_map(per_device, mesh=mesh, in_specs=in_specs, out_specs=out_specs, check_vma=False)
```

```python
import functools

import jax
import jax.numpy as jnp
from jax import lax
from jax.experimental import pallas as pl
from jax.experimental.pallas import tpu as pltpu
from jax.sharding import PartitionSpec as P

VMEM = pl.BlockSpec(memory_space=pltpu.VMEM)
SMEM = pl.BlockSpec(memory_space=pltpu.SMEM)
HBM = pl.BlockSpec(memory_space=pltpu.HBM)
BF16 = jnp.bfloat16
F32 = jnp.float32
LIMIT = 2 << 20


def held(array):
    return pltpu.with_memory_space_constraint(array, pltpu.VMEM)


def assemble_kernel(*refs):
    *pieces, out, stage, arrived, left = refs
    count = len(pieces) // 2
    copies = []
    for i in range(2):
        at = 0
        for piece in pieces[i * count : (i + 1) * count]:
            rows, columns = piece.shape
            here = (pl.ds(at, rows), pl.ds(i * columns, columns))
            n = len(copies)
            copies.append(
                (
                    pltpu.make_async_copy(piece, stage.at[here], arrived.at[n]),
                    pltpu.make_async_copy(stage.at[here], out.at[here], left.at[n]),
                )
            )
            at += rows
    for into, _ in copies:
        into.start()
    for into, onward in copies:
        into.wait()
        onward.start()
    for _, onward in copies:
        onward.wait()


def assemble(lefts, rights):
    pieces = [pltpu.with_memory_space_constraint(piece, pltpu.HBM) for piece in lefts + rights]
    shape = (sum(piece.shape[0] for piece in lefts), 2 * lefts[0].shape[1])
    return pl.pallas_call(
        assemble_kernel,
        out_shape=pltpu.HBM(shape, BF16),
        in_specs=[HBM] * len(pieces),
        out_specs=HBM,
        scratch_shapes=[pltpu.VMEM(shape, BF16)] + [pltpu.SemaphoreType.DMA((len(pieces),))] * 2,
        compiler_params=pltpu.CompilerParams(vmem_limit_bytes=16 << 20),
        name="assemble",
    )(*pieces)


def place_kernel(layouts, state, *rest):
    weights, sems = rest[-3], rest[-1]
    row, col = state[2], state[3]
    height = weights.shape[1] // 32
    copies = []
    for source, (slot, shifts) in zip(rest, layouts):
        for i, shift in enumerate(shifts):
            for j, across in enumerate((0, -1, 1, -2)):
                replica = lax.rem(row + across + 4, 4) * 8 + lax.rem(col + shift + 8, 8)
                into = weights.at[slot, pl.ds(pl.multiple_of(replica * height, 16), height), :]
                at = (i * 4 + j) * height
                copies.append(pltpu.make_async_copy(source.at[at : at + height, :], into, sems.at[len(copies)]))
    for copy in copies:
        copy.start()
    for copy in copies:
        copy.wait()


def place(state, layouts, pieces, buffers):
    width = pieces[0].shape[1]
    pieces = [pltpu.with_memory_space_constraint(piece, pltpu.HBM) for piece in pieces]
    copies = 4 * sum(len(shifts) for _, shifts in layouts)
    return pl.pallas_call(
        functools.partial(place_kernel, layouts),
        out_shape=[pltpu.VMEM((2, width, width), BF16)] * 2,
        in_specs=[SMEM] + [HBM] * len(pieces) + [VMEM] * len(buffers),
        out_specs=[VMEM] * 2,
        input_output_aliases={1 + len(pieces) + i: i for i in range(len(buffers))},
        scratch_shapes=[pltpu.SemaphoreType.DMA((copies,))],
        compiler_params=pltpu.CompilerParams(vmem_limit_bytes=LIMIT),
        name="place_weight",
    )(state, *pieces, *[held(b) for b in buffers])


def pack_kernel(collected, totals, packed):
    parts, rows = collected.shape[1:3]
    for m in range(parts):
        packed[m * rows : (m + 1) * rows, :] = collected[1, m]
    total = totals[1]
    head = total.astype(BF16).astype(F32)
    row = lax.broadcasted_iota(jnp.int32, (16, total.shape[1]), 0)
    tail = jnp.where(row == 0, head, jnp.where(row == 1, total - head, 0.0))
    packed[parts * rows :, :] = tail.astype(BF16)


def pack(collected, totals):
    _, parts, rows, width = collected.shape
    return pl.pallas_call(
        pack_kernel,
        out_shape=jax.ShapeDtypeStruct((parts * rows + 16, width), BF16),
        in_specs=[VMEM] * 2,
        out_specs=VMEM,
        compiler_params=pltpu.CompilerParams(vmem_limit_bytes=LIMIT),
        name="pack",
    )(held(collected), held(totals))


def transpose_kernel(early, state, weights, _, turned):
    step = 256
    count = weights.shape[1] // step

    @pl.when((state[0] <= 1) == early)
    def _():
        def turn(i, _):
            rows = pl.ds(pl.multiple_of(i * step, step), step)
            for slot in range(2):
                for j in range(0, count * step, step):
                    turned[slot, j : j + step, rows] = weights[slot, rows, j : j + step].T

        lax.fori_loop(0, count, turn, None)


def transpose(early, state, weights, turned):
    return pl.pallas_call(
        functools.partial(transpose_kernel, early),
        out_shape=pltpu.VMEM(weights.shape, BF16),
        in_specs=[SMEM] + [VMEM] * 2,
        out_specs=VMEM,
        input_output_aliases={2: 0},
        compiler_params=pltpu.CompilerParams(vmem_limit_bytes=LIMIT),
        name="transpose_weight",
    )(state, held(weights), held(turned))


def normalize(acts):
    values = acts.astype(F32)
    center = values - jnp.mean(values, axis=-1, keepdims=True)
    variance = jnp.mean(center * center, axis=-1, keepdims=True)
    inverse = 1.0 / jnp.sqrt(variance + 1e-05)
    return center * inverse, inverse


def project(x, gain, weight_ref, into, scaled):
    normed, _ = normalize(x)
    scaled[...] = (normed * gain).astype(BF16)
    width = weight_ref.shape[1]
    tile = width // 2
    for i in range(0, width, tile):
        here = slice(i, i + tile)
        product = jnp.dot(scaled[...], weight_ref[:, here], preferred_element_type=F32)
        into[:, here] = (x[:, here].astype(F32) + product).astype(BF16)


def pull_back(grad, x, gain, turned_ref, into, total, back):
    width = turned_ref.shape[1]
    tile = width // 2
    for i in range(0, width, tile):
        here = slice(i, i + tile)
        back[:, here] = jnp.dot(grad, turned_ref[:, here], preferred_element_type=F32)
    normed, inverse = normalize(x)
    back_proj = back[...]
    scaled = back_proj * gain
    mean_one = jnp.mean(scaled, axis=-1, keepdims=True)
    mean_two = jnp.mean(scaled * normed, axis=-1, keepdims=True)
    norm_grad = inverse * (scaled - mean_one - normed * mean_two)
    into[...] = (grad.astype(F32) + norm_grad).astype(BF16)
    total[...] = total[...] + jnp.sum(back_proj * normed, axis=0, keepdims=True)


def forward_kernel(k, part, state, arrived, gains, weights, *rest):
    sent, stash, scaled = rest[-3:]
    core = state[1]

    @pl.when(state[0] == k)
    def _():
        x = arrived[...]
        stash[part, 0] = x
        project(x, gains[0:1, :], weights.at[core], stash.at[part, 1], scaled)
        project(stash[part, 1], gains[1:2, :], weights.at[1 - core], sent, scaled)


def forward(k, part, parts, state, arrived, gains, weights, turned, stash):
    operands = [state, arrived, gains, held(weights), held(turned)] + [held(b) for b in stash]
    return pl.pallas_call(
        functools.partial(forward_kernel, k, part),
        out_shape=[
            jax.ShapeDtypeStruct(arrived.shape, BF16),
            pltpu.VMEM((parts, 2) + arrived.shape, BF16),
        ],
        in_specs=[SMEM] + [VMEM] * (len(operands) - 1),
        out_specs=[VMEM] * 2,
        input_output_aliases={5: 1} if stash else {},
        scratch_shapes=[pltpu.VMEM(arrived.shape, BF16)],
        compiler_params=pltpu.CompilerParams(vmem_limit_bytes=LIMIT),
        name="forward",
    )(*operands)


def turn_kernel(part, stages, state, fresh, received, gains, weights, turned, *rest):
    sent, collected, totals, scaled, middle, back = rest[-6:]
    stage, core = state[0], state[1]
    if part == 0:
        totals[...] = jnp.zeros_like(totals)

    @pl.when(stage == stages - 1)
    def _():
        x = received[...]
        project(x, gains[0:1, :], weights.at[core], middle, scaled)
        pull_back(
            fresh[...], middle[...], gains[1:2, :], turned.at[1 - core], collected.at[1 - core, part], totals.at[1 - core], back
        )
        pull_back(collected[1 - core, part], x, gains[0:1, :], turned.at[core], sent, totals.at[core], back)
        collected[core, part] = sent[...]


def backward_kernel(k, part, state, received, stash, gains, turned, *rest):
    sent, collected, totals, back = rest[-4:]
    core = state[1]

    @pl.when(state[0] == k)
    def _():
        pull_back(
            received[...], stash[part, 1], gains[1:2, :], turned.at[1 - core], collected.at[1 - core, part], totals.at[1 - core], back
        )
        pull_back(collected[1 - core, part], stash[part, 0], gains[0:1, :], turned.at[core], sent, totals.at[core], back)
        collected[core, part] = sent[...]


def backward(kernel, parts, operands, kept, scratch, name):
    rows, width = operands[1].shape
    count = len(operands)
    return pl.pallas_call(
        kernel,
        out_shape=[
            jax.ShapeDtypeStruct((rows, width), BF16),
            pltpu.VMEM((2, parts, rows, width), BF16),
            pltpu.VMEM((2, 1, width), F32),
        ],
        in_specs=[SMEM] + [VMEM] * (count + len(kept) - 1),
        out_specs=[VMEM] * 3,
        input_output_aliases={count + i: 1 + i for i in range(len(kept))},
        scratch_shapes=scratch + [pltpu.VMEM((rows, width), F32)],
        compiler_params=pltpu.CompilerParams(vmem_limit_bytes=LIMIT),
        name=name,
    )(*operands, *[held(b) for b in kept])


def per_device(inputs, cotangent, weight, gain, momentum, prev_grads):
    sections = lax.axis_size("section")
    section = lax.axis_index("section")
    stages = sections // 2
    stage, core = section // 2, lax.rem(section, 2)
    batches, rows, width = inputs.shape
    parts = batches // 2
    siblings = [(i, i ^ 1) for i in range(sections)]

    def swap(array):
        return lax.ppermute(array, "section", siblings)

    def ordered(own, other):
        return jnp.where(core == 0, jnp.concatenate([own, other], 0), jnp.concatenate([other, own], 0))

    def unpacked(block):
        return block[0:1].astype(F32) + block[1:2].astype(F32)

    def over(array, rows, columns):
        pairs = [
            (y * 8 + z, ((y + rows) % 4) * 8 + (z + columns) % 8) for y in range(4) for z in range(8)
        ]
        return lax.ppermute(array, "dp", pairs)

    def first_block(shard):
        above, below = over(shard, 1, 0), over(shard, -1, 0)
        return jnp.concatenate([shard, above, below, over(above, 1, 0)], 0)

    half = width // 2
    shards = [weight[0, :, :half], weight[0, :, half:]]
    block = first_block(shards[0])
    shards[1], block = lax.optimization_barrier((shards[1], block))
    blocks = [block, first_block(shards[1])]
    rings = [[(block, block)] for block in blocks]
    for step in range(3):
        for ring in rings:
            right, left = ring[-1]
            ring.append(lax.optimization_barrier((over(right, 0, 1), over(left, 0, -1))))
    ends = [over(rings[0][3][0], 0, 1), over(rings[1][3][1], 0, -1)]
    inner = [[ring[0][0], *ring[1], *ring[2]] for ring in rings]
    inner, rings[0][3], rings[1][3] = lax.optimization_barrier((inner, rings[0][3], rings[1][3]))
    inner = assemble(*inner)
    inner_other = swap(inner)
    own_gain, inner = lax.optimization_barrier((gain, inner))
    gains = ordered(gain, swap(own_gain))
    ends, gains = lax.optimization_barrier((ends, gains))

    bucket, inner_other = lax.optimization_barrier((prev_grads[0, 0].astype(BF16), inner_other))
    pieces = lax.all_to_all(bucket, "dp", 0, 0, tiled=True).astype(F32)
    summed = jnp.sum(pieces, axis=0, keepdims=True)
    new_momentum = 0.9 * momentum + (summed / lax.axis_size("dp"))[None]


    ends, new_momentum = lax.optimization_barrier((ends, new_momentum))
    outer = assemble(*[[*ring[3], end] for ring, end in zip(rings, ends)])
    outer_other = swap(outer)

    replica = lax.axis_index("dp")
    state = jnp.stack([stage, core, replica // 8, lax.rem(replica, 8)]).astype(jnp.int32)
    fresh = lax.dynamic_slice_in_dim(inputs, core * parts, parts, 0)
    target = lax.dynamic_slice_in_dim(cotangent, core * parts, parts, 0)
    fresh = [fresh[m] for m in range(parts)]
    target = [target[m] for m in range(parts)]
    gains, state, fresh, target, outer, new_momentum = lax.optimization_barrier(
        (gains, state, fresh, target, outer, new_momentum)
    )
    near, far = (0, -1, 1, -2, 2), (-3, 3, 4)
    buffers = place(state, ((0, near), (0, far), (1, near)), [inner, outer, inner_other], [])
    weights, turned = place(state, ((1, far),), [outer_other], buffers)
    turned = transpose(False, state, weights, turned)

    def hop(array, k, to, after):
        if after is not None:
            array, after = lax.optimization_barrier((array, after))
        return lax.ppermute(array, "section", [(2 * k + c, 2 * to + c) for c in range(2)])

    arrived = fresh
    stash, kept = [], []
    for k in range(stages - 1):
        landed = []
        for m in range(parts):
            sent, *stash = forward(k, m, parts, state, arrived[m], gains, weights, turned, stash)
            landed.append(hop(sent, k, k + 1, landed[-1] if landed else None))
        arrived = landed
        if k == 3:
            turned = transpose(True, state, weights, turned)
    for k in range(stages - 1, -1, -1):
        landed = []
        for m in range(parts):
            if k == stages - 1:
                kernel, scratch = functools.partial(turn_kernel, m, stages), [pltpu.VMEM((rows, width), BF16)] * 2
                operands = [state, target[m], arrived[m], gains, held(weights), held(turned)]
            else:
                kernel, scratch = functools.partial(backward_kernel, k, m), []
                operands = [state, arrived[m], held(stash[0]), gains, held(turned), held(weights)]
            leaving, *kept = backward(kernel, parts, operands, kept, scratch, "turn" if scratch else "backward")
            if k > 0:
                landed.append(hop(leaving, k, k - 1, landed[-1] if landed else None))
        arrived = landed
    collected, totals = kept

    other = swap(pack(collected, totals))
    input_grads = ordered(collected[0], other[: parts * rows].reshape(parts, rows, width))[None]
    gain_grads = (totals[0] + unpacked(other[parts * rows :]))[None]

    return input_grads, gain_grads, new_momentum


def solution(mesh):
    in_specs = (
        P(None, "dp", None),
        P(None, "dp", None),
        P("section", "dp", None),
        P("section", None),
        P("section", "dp", None),
        P("section", "dp", None, None),
    )
    out_specs = (P("section", None, "dp", None), P("section", "dp", None), P("section", "dp", None))
    return jax.shard_map(per_device, mesh=mesh, in_specs=in_specs, out_specs=out_specs, check_vma=False)
```
